128 devices in a mesh: seq: 128 (over y, x, z, core).
Axes of the slice: x: 4, y: 4, z: 4, core: 2. Of those that a mesh axis runs over, the one named last changes fastest.
Arguments:
- queries: bfloat16 [131072, 1024], P('seq'), may hold values from -8 to 8, as said below
- keys: bfloat16 [131072, 1024], P('seq'), may hold values from -8 to 8
- values: bfloat16 [131072, 1024], P('seq'), may hold values from -6 to 6
- w_out: bfloat16 [1024, 2048], replicated, may hold values from -0.1875 to 0.1875
Outputs:
- output: bfloat16 [131072, 2048], P('seq')
The draws below stay inside these ranges and needn't reach their ends.
Inputs may be any that keep to these rules, and one draw needn't show every extreme that they name: `queries`: query entries lie in the range.
All inputs are finite; a program needn't handle non-finite values.
Results may differ from the reference program's by a relative error of at most 0.0023.
The reference program's roundings to bfloat16 on the way count: a program that leaves them out, or rounds other values in their place, can miss the bound.
Values may be sent and summed in bfloat16 or wider, within the bound.
A program may use at most 128 MiB of HBM per device.

```python
import jax
import jax.numpy as jnp
from jax import lax

HEADS = 8
HEAD_DIM = 128
D_MODEL = 2048
BLOCK = 256
TOK_DEV = 1024
SEQ = 131072
LEVELS = 8
WIDTH = 1024


def draw_queries(key, part):
    key = jax.random.fold_in(key, 11)
    base = jnp.clip(jax.random.normal(key, (SEQ, HEADS * HEAD_DIM), jnp.float32), -4.0, 4.0)
    return base.astype(jnp.bfloat16)


def draw_keys(key, part):
    key = jax.random.fold_in(key, 23)
    base = jnp.clip(jax.random.normal(key, (SEQ, HEADS * HEAD_DIM), jnp.float32), -4.0, 4.0)
    return base.astype(jnp.bfloat16)


def steps_of(own_key, shape, shards, low, largest):
    def one(dim, shards_of):
        draws = jax.random.uniform(jax.random.fold_in(jax.random.fold_in(own_key, 6), dim), (shards_of,), jnp.float32, low / len(shards), largest / len(shards))
        return jnp.repeat(jnp.exp(draws), shape[dim] // shards_of).reshape((-1,) + (1,) * (len(shape) - dim - 1))

    factor_of = one(*shards[0])
    for cut in shards[1:]:
        factor_of = factor_of * one(*cut)
    return factor_of


def centred(stream_key, extent, scale, limit, pieces=(), kind=jnp.bfloat16):
    values = scale * jax.random.normal(stream_key, extent, jnp.float32)
    if pieces:
        values = values * steps_of(stream_key, extent, pieces, -0.22, 0.18)
    return jnp.clip(values, -limit, limit).astype(kind)


def setup_inputs(seed: int = 0) -> dict:
    splits = jax.random.split(jax.random.key(seed), 5)
    queries = draw_queries(jax.random.fold_in(splits[4], 71), 0)
    keys = draw_keys(jax.random.fold_in(splits[4], 71), 0)
    values = centred(splits[2], (SEQ, WIDTH), 1.0, 6.0, ((0, 128),))
    w_out = centred(splits[3], (WIDTH, D_MODEL), WIDTH ** -0.5, 0.1875)
    return {"queries": queries, "keys": keys, "values": values, "w_out": w_out}


NEG = -1e30


def block_term(query_rows, key_rows, value_rows, allowed, factor):
    count_q = query_rows.shape[0]
    count_k = key_rows.shape[0]
    q_heads = query_rows.reshape(count_q, HEADS, HEAD_DIM).astype(jnp.float32)
    k_heads = key_rows.reshape(count_k, HEADS, HEAD_DIM).astype(jnp.float32)
    v_heads = value_rows.reshape(count_k, HEADS, HEAD_DIM).astype(jnp.float32)
    scores = jnp.einsum("ghd,khd->hgk", q_heads, k_heads) * (HEAD_DIM ** -0.5)
    scores = jnp.where(allowed[None], scores, NEG)
    peak = jnp.max(scores, axis=-1)
    probs = jnp.exp(scores - peak[..., None])
    total = factor * jnp.sum(probs, axis=-1)
    rounded = lax.optimization_barrier(probs.astype(jnp.bfloat16)).astype(jnp.float32)
    weighted = factor * jnp.einsum("hgk,khd->ghd", rounded, v_heads)
    return weighted.reshape(count_q, HEADS * HEAD_DIM), peak.T, total.T


def level_zero(q_rows, k_rows, v_rows):
    count = q_rows.shape[0]
    pairs = count // (2 * BLOCK)
    index = jnp.arange(2 * BLOCK)
    causal = index[None, :] <= index[:, None]
    width = HEADS * HEAD_DIM
    fn = jax.vmap(lambda a, b, c: block_term(a, b, c, causal, 1.0))
    num, peak, total = fn(q_rows.reshape(pairs, 2 * BLOCK, width), k_rows.reshape(pairs, 2 * BLOCK, width),
                          v_rows.reshape(pairs, 2 * BLOCK, width))
    return num.reshape(count, width), peak.reshape(count, HEADS), total.reshape(count, HEADS)


def coarse_level(coarse_q, coarse_k, coarse_v, start, count, level):
    group = min(count, BLOCK)
    blocks = count // group
    offsets = start + jnp.arange(blocks, dtype=jnp.int32) * group
    allowed = jnp.ones((group, BLOCK), dtype=bool)

    def one(offset):
        query_rows = lax.dynamic_slice_in_dim(coarse_q, offset, group, 0)
        index = offset // BLOCK
        key_start = (jnp.maximum(index - 1, 0) * BLOCK).astype(jnp.int32)
        key_rows = lax.dynamic_slice_in_dim(coarse_k, key_start, BLOCK, 0)
        value_rows = lax.dynamic_slice_in_dim(coarse_v, key_start, BLOCK, 0)
        num, peak, total = block_term(query_rows, key_rows, value_rows, allowed, float(2 ** level))
        live = index % 2 == 1
        return jnp.where(live, num, 0.0), jnp.where(live, peak, NEG), jnp.where(live, total, 0.0)

    num, peak, total = jax.vmap(one)(offsets)
    return num.reshape(count, -1), peak.reshape(count, HEADS), total.reshape(count, HEADS)


def combine(terms, count):
    peaks = [jnp.repeat(term[1], 2 ** term[3], axis=0) for term in terms]
    top = peaks[0]
    for item in peaks[1:]:
        top = jnp.maximum(top, item)
    acc_num = jnp.zeros((count, HEADS, HEAD_DIM), jnp.float32)
    acc_den = jnp.zeros((count, HEADS), jnp.float32)
    for term, fine_peak in zip(terms, peaks):
        factor = jnp.exp(fine_peak - top)
        fine_num = jnp.repeat(term[0], 2 ** term[3], axis=0).reshape(count, HEADS, HEAD_DIM)
        acc_num = acc_num + factor[:, :, None] * fine_num
        acc_den = acc_den + factor * jnp.repeat(term[2], 2 ** term[3], axis=0)
    return (acc_num / acc_den[:, :, None]).reshape(count, HEADS * HEAD_DIM).astype(jnp.bfloat16)


def reference(queries, keys, values, w_out):
    width = HEADS * HEAD_DIM
    coarse = []
    for level in range(1, LEVELS + 1):
        trio = []
        for source in (queries, keys, values):
            summed = jnp.sum(source.reshape(SEQ >> level, 2 ** level, width), axis=1, dtype=jnp.float32)
            trio.append((summed / (2 ** level)).astype(jnp.bfloat16))
        coarse.append(trio)

    def stretch(index):
        start = (index * TOK_DEV).astype(jnp.int32)
        q_rows = lax.dynamic_slice_in_dim(queries, start, TOK_DEV, 0)
        k_rows = lax.dynamic_slice_in_dim(keys, start, TOK_DEV, 0)
        v_rows = lax.dynamic_slice_in_dim(values, start, TOK_DEV, 0)
        terms = [level_zero(q_rows, k_rows, v_rows) + (0,)]
        for level in range(1, LEVELS + 1):
            count = TOK_DEV >> level
            trio = coarse[level - 1]
            terms.append(coarse_level(trio[0], trio[1], trio[2], (index * count).astype(jnp.int32), count, level) + (level,))
        attended = combine(terms, TOK_DEV)
        return jnp.dot(attended, w_out, preferred_element_type=jnp.float32).astype(jnp.bfloat16)

    result = lax.map(stretch, jnp.arange(SEQ // TOK_DEV, dtype=jnp.int32))
    return result.reshape(SEQ, D_MODEL)
```

```python
import functools
import math

import jax
import jax.numpy as jnp
from jax import lax
from jax.experimental import pallas as pl
from jax.experimental.pallas import tpu as pltpu
from jax.sharding import PartitionSpec as P

MESH = pl.DeviceIdType.MESH
HEAD = 128
PAIRS = 4
WIDE = 256
NEG = -1e30
C2 = HEAD ** -0.5 * math.log2(math.e)
BF = jnp.bfloat16
F32 = jnp.float32


def nt_dot(a, b):
    return lax.dot_general(a, b, (((1,), (1,)), ((), ())), preferred_element_type=F32)


def dot(a, b):
    return lax.dot_general(a, b, (((1,), (0,)), ((), ())), preferred_element_type=F32)


def coarse_term(q, k, v, level, flag):
    unit = 4.0 ** -level
    s = nt_dot(q, k)
    m = jnp.max(s, axis=1, keepdims=True)
    p = jnp.exp2((s - m) * (C2 * unit))
    num = dot(p.astype(BF), v)
    total = jnp.broadcast_to(jnp.sum(p, axis=1, keepdims=True) * 2.0 ** level, num.shape)
    peak = jnp.broadcast_to(m * unit, num.shape)
    if flag is None:
        return num, peak, total
    return jnp.where(flag, num, 0.0), jnp.where(flag, peak, NEG), jnp.where(flag, total, 0.0)


def merge(a, b):
    top = jnp.maximum(a[1], b[1])
    fa = jnp.exp2((a[1] - top) * C2)
    fb = jnp.exp2((b[1] - top) * C2)
    return fa * a[0] + fb * b[0], top, fa * a[2] + fb * b[2]


def widen(state, ref, times, start=0):
    rows = state[0].shape[0]
    for plane, value in enumerate(state):
        for r in range(times):
            ref[plane, pl.ds(start + r, rows, stride=times), :] = value
    return tuple(ref[i, pl.ds(start, rows * times), :] for i in range(3))


def local_block(q, k, v, init, bias, half):
    s = [nt_dot(q, k[i * 256:(i + 1) * 256]) for i in range(half + 1)]
    s[half] = s[half] + bias
    m = init[1]
    for item in s:
        m = jnp.maximum(m, jnp.max(item, axis=1, keepdims=True))
    m2 = jnp.concatenate([m, m], axis=1)
    f = jnp.exp2((init[1] - m) * C2)
    num, total = f * init[0], f * init[2]
    sums = None
    for i, item in enumerate(s):
        p = jnp.exp2((item - m2) * C2)
        num = num + dot(p.astype(BF), v[i * 256:(i + 1) * 256])
        sums = p if sums is None else sums + p
    return num, m, total + jnp.sum(sums, axis=1, keepdims=True)


def kernel(q_hbm, k_hbm, v_hbm, att_hbm, qb, kb, vb, pool, bias,
           kv1, q1, kv2, q2, r2, kv3, q3, r3, kv4, q4, r4,
           ts, rt, xs, r5, r6, r7, r8, cs, cr, wide, base, outb,
           load_sem, out_sem, s2, g2, s3, g3, y3, z3, s4, g4, y4, z4,
           sa, ga, sb, gb, sc, gc):
    me = lax.axis_index("seq")
    core = me & 1
    own = me & 7
    octet = me - own

    def bit(i):
        return (me >> i) & 1

    def load(hp, t):
        src = (k_hbm, v_hbm, q_hbm)[t]
        dst = (kb, vb, qb)[t]
        cols = pl.ds(pl.multiple_of(hp * WIDE, WIDE), WIDE)
        return pltpu.make_async_copy(src.at[:, cols], dst.at[hp], load_sem.at[hp, t])

    for hp in range(PAIRS):
        for t in range(3):
            load(hp, t).start()

    barrier = pltpu.get_barrier_semaphore()
    masks = list(range(1, 8)) + [8 * o for o in range(1, 16)]

    def greet(i, _):
        mask = jnp.where(i < 8, i, (i - 7) * 8)
        pl.semaphore_signal(barrier, inc=1, device_id=(me ^ mask,), device_id_type=MESH)
        return 0

    lax.fori_loop(1, 23, greet, 0)

    row = lax.broadcasted_iota(jnp.int32, (304, WIDE), 0)
    col = lax.broadcasted_iota(jnp.int32, (304, WIDE), 1)
    tail = row >= 240
    shift = jnp.where(row < 128, 1, jnp.where(row < 192, 2, jnp.where(row < 224, 3, 4)))
    off = jnp.where(row < 128, row, jnp.where(row < 192, row - 128, jnp.where(row < 224, row - 192, row - 224)))
    t = row - 240
    shift_t = jnp.where(t < 32, 5, jnp.where(t < 48, 6, jnp.where(t < 56, 7, 8)))
    off_t = jnp.where(t < 32, t, jnp.where(t < 48, t - 32, jnp.where(t < 56, t - 48, t - 56)))
    shift = jnp.where(tail, shift_t, shift)
    off = jnp.where(tail, off_t, off)
    for i in range(4):
        at = jnp.where(tail, col + 256 * i, col)
        pool[i] = jnp.where((at >> shift) == off, 1.0, 0.0).astype(BF)
    r_i = lax.broadcasted_iota(jnp.int32, (256, 256), 0)
    c_i = lax.broadcasted_iota(jnp.int32, (256, 256), 1)
    bias[...] = jnp.where(c_i <= r_i, 0.0, NEG)

    tr = lax.broadcasted_iota(jnp.int32, (64, WIDE), 0)
    side = jnp.where(tr < 32, bit(3), jnp.where(tr < 48, bit(4), jnp.where(tr < 56, bit(5), bit(6))))

    pl.semaphore_wait(barrier, len(masks))

    def copy_to(src, dst, send, recv, device):
        return pltpu.make_async_remote_copy(src_ref=src, dst_ref=dst, send_sem=send, recv_sem=recv,
                                            device_id=(device,), device_id_type=MESH)

    def send2(hp):
        return copy_to(kv2.at[hp], r2.at[hp], s2.at[hp], g2.at[hp], me ^ 1)

    def send3(hp):
        return copy_to(kv3.at[hp], r3.at[hp, core], s3.at[hp], g3.at[hp], me ^ 2)

    def relay3(hp):
        return copy_to(r3.at[hp, core], r3.at[hp, core], y3.at[hp], z3.at[hp], me ^ 1)

    def send4(hp, j):
        mask = 4 + 2 * j
        return copy_to(kv4.at[hp], r4.at[hp, core, bit(1)], s4.at[hp, j], g4.at[hp, j], me ^ mask)

    def recv4(hp, j):
        slot = bit(1) ^ j
        mask = 4 + 2 * j
        return copy_to(kv4.at[hp], r4.at[hp, core, slot], s4.at[hp, j], g4.at[hp, j], me ^ mask)

    def relay4(hp):
        return copy_to(r4.at[hp, core], r4.at[hp, core], y4.at[hp], z4.at[hp], me ^ 1)

    def send_a(h):
        return copy_to(ts.at[h], rt.at[own], sa.at[h], ga.at[own], octet + h)

    def recv_a(h):
        return copy_to(ts.at[h], rt.at[h], sa.at[h], ga.at[h], octet + h)

    def send_c(h):
        return copy_to(cs.at[h], cr.at[own], sc.at[h], gc.at[own], octet + h)

    def recv_c(h):
        return copy_to(cs.at[h], cr.at[h], sc.at[h], gc.at[h], octet + h)

    def copy_b(level, i):
        count = 256 >> (level - 5)
        start = (0, 256, 384, 448)[level - 5]
        n = 1 << (level - 5)
        dst = (r5, r6, r7, r8)[level - 5]
        slot = n - 1 + i
        mask = 8 * (n + i)
        return copy_to(xs.at[:, pl.ds(start, count)], dst.at[i], sb.at[slot], gb.at[slot], me ^ mask)

    def pool_pair(hp, _):
        tails = []
        for t in range(3):
            load(hp, t).wait()
            src = (kb, vb, qb)[t]
            acc = None
            for i in range(4):
                y = dot(pool[i], src[hp, i * 256:(i + 1) * 256, :])
                yb = y[:240].astype(BF)
                if t < 2:
                    if i < 2:
                        kv1[hp, t, i * 128:(i + 1) * 128, :] = yb[:128]
                    kv2[hp, t, i * 64:(i + 1) * 64, :] = yb[128:192]
                    kv3[hp, t, i * 32:(i + 1) * 32, :] = yb[192:224]
                    kv4[hp, t, i * 16:(i + 1) * 16, :] = yb[224:240]
                else:
                    if i >= 2:
                        q1[hp, (i - 2) * 128:(i - 1) * 128, :] = yb[:128]
                    q2[hp, i * 64:(i + 1) * 64, :] = yb[128:192]
                    q3[hp, i * 32:(i + 1) * 32, :] = yb[192:224]
                    q4[hp, i * 16:(i + 1) * 16, :] = yb[224:240]
                acc = y[240:] if acc is None else acc + y[240:]
            tails.append(acc)
        first = jnp.where(side == 0, tails[0], tails[2]).astype(BF)
        second = tails[1].astype(BF)
        for e in range(2):
            h = 2 * hp + e
            ts[h, 0] = first[:, e * HEAD:(e + 1) * HEAD]
            ts[h, 1] = second[:, e * HEAD:(e + 1) * HEAD]

            @pl.when(h != own)
            def _():
                send_a(h).start()

        @pl.when(bit(2) == 0)
        def _():
            send4(hp, 0).start()
            send4(hp, 1).start()

        @pl.when(bit(1) == 0)
        def _():
            send3(hp).start()

        @pl.when(core == 0)
        def _():
            send2(hp).start()

        return 0

    lax.fori_loop(0, PAIRS, pool_pair, 0)
    rt[own] = ts[own]

    def wait_a():
        def one(h, _):
            @pl.when(h != own)
            def _():
                recv_a(h).wait_recv()
            return 0
        lax.fori_loop(0, 8, one, 0)
        i = lax.broadcasted_iota(jnp.int32, (512, 512), 0)
        j = lax.broadcasted_iota(jnp.int32, (512, 512), 1)
        i6, i7, i8 = i - 256, i - 384, i - 448
        at = jnp.where(i < 256, (i >> 5) * 64 + (i & 31),
             jnp.where(i < 384, (i6 >> 4) * 64 + 32 + (i6 & 15),
             jnp.where(i < 448, (i7 >> 3) * 64 + 48 + (i7 & 7),
             jnp.where(i < 480, (i8 >> 2) * 64 + 56 + (i8 & 3), -1))))
        move = jnp.where(at == j, 1.0, 0.0).astype(BF)
        both = jnp.concatenate([rt[:, 0].reshape(512, HEAD), rt[:, 1].reshape(512, HEAD)], axis=1)
        x = dot(move, both).astype(BF)
        xs[0] = x[:, :HEAD]
        xs[1] = x[:, HEAD:]
        for level in range(8, 4, -1):
            n = 1 << (level - 5)

            @pl.when(bit(level - 2) == 0)
            def _():
                for i in range(n):
                    copy_b(level, i).start()

    def wait_b():
        for level in range(8, 4, -1):
            n = 1 << (level - 5)

            @pl.when(bit(level - 2) == 1)
            def _():
                for i in range(n):
                    copy_b(level, i).wait_recv()
        terms = []
        for level, ref in ((8, r8), (7, r7), (6, r6), (5, r5)):
            start = (0, 256, 384, 448)[level - 5]
            rows = 256 >> (level - 5)
            terms.append(coarse_term(xs[0, start:start + rows, :], ref[:, 0].reshape(256, HEAD),
                                     ref[:, 1].reshape(256, HEAD), level, bit(level - 2) == 1))
        state = terms[0]
        for term in terms[1:]:
            state = merge(widen(state, wide.at[0], 2), term)
        lane = lax.broadcasted_iota(jnp.int32, (256, HEAD), 1)
        cs[:, 0] = state[0].reshape(8, 32, HEAD)
        cs[:, 1] = jnp.where(lane < 64, state[1], state[2]).reshape(8, 32, HEAD)
        cr[own] = cs[own]

        def one(h, _):
            @pl.when(h != own)
            def _():
                send_c(h).start()
            return 0
        lax.fori_loop(0, 8, one, 0)

    def local_pair(hp, _):
        @pl.when(core == 1)
        def _():
            send2(hp).wait_recv()
        for e in range(2):
            cols = slice(e * HEAD, (e + 1) * HEAD)
            two = coarse_term(q2[hp, :, cols], r2[hp, 0, :, cols], r2[hp, 1, :, cols], 2, core == 1)
            one = coarse_term(q1[hp, :, cols], kv1[hp, 0, :, cols], kv1[hp, 1, :, cols], 1, None)
            w = wide.at[e]
            low = tuple(x[:128] for x in two)
            high = tuple(x[128:] for x in two)
            init0 = widen(low, w, 4)
            init1 = widen(merge(widen(high, w, 2, 512), one), w, 2, 512)
            for seg, init in ((0, init0), (1, init1)):
                k = kb[hp, seg * 512:(seg + 1) * 512, cols]
                v = vb[hp, seg * 512:(seg + 1) * 512, cols]
                for half in range(2):
                    at = seg * 512 + half * 256
                    q = qb[hp, at:at + 256, cols]
                    part = tuple(x[half * 256:(half + 1) * 256] for x in init)
                    res = local_block(q, k, v, part, bias[...], half)
                    for i in range(3):
                        base[2 * hp + e, i, at:at + 256, :] = res[i]

        @pl.when(hp == 0)
        def _():
            wait_a()

        @pl.when(hp == 2)
        def _():
            wait_b()
        return 0

    lax.fori_loop(0, PAIRS, local_pair, 0)

    def recv_c_all(h, _):
        @pl.when(h != own)
        def _():
            recv_c(h).wait_recv()
        return 0

    lax.fori_loop(0, 8, recv_c_all, 0)

    def out_copy(hp):
        cols = pl.ds(pl.multiple_of(hp * WIDE, WIDE), WIDE)
        return pltpu.make_async_copy(outb.at[hp], att_hbm.at[:, cols], out_sem.at[hp])

    def final_pair(step, _):
        @pl.when(step < PAIRS)
        def _():
            @pl.when(bit(2) == 1)
            def _():
                recv4(step, 0).wait_recv()
                recv4(step, 1).wait_recv()
                relay4(step).start()

            @pl.when(bit(1) == 1)
            def _():
                send3(step).wait_recv()
                relay3(step).start()

        @pl.when(step > 0)
        def _():
            hp = step - 1

            @pl.when(bit(2) == 1)
            def _():
                copy_to(r4.at[hp, 1 - core], r4.at[hp, 1 - core], y4.at[hp], z4.at[hp], me ^ 1).wait_recv()

            @pl.when(bit(1) == 1)
            def _():
                copy_to(r3.at[hp, 1 - core], r3.at[hp, 1 - core], y3.at[hp], z3.at[hp], me ^ 1).wait_recv()

            for e in range(2):
                cols = slice(e * HEAD, (e + 1) * HEAD)
                h = 2 * hp + e
                w = wide.at[e]
                three = coarse_term(q3[hp, :, cols], r3[hp, :, 0, :, cols].reshape(256, HEAD),
                                    r3[hp, :, 1, :, cols].reshape(256, HEAD), 3, bit(1) == 1)
                four = coarse_term(q4[hp, :, cols], r4[hp, :, :, 0, :, cols].reshape(256, HEAD),
                                   r4[hp, :, :, 1, :, cols].reshape(256, HEAD), 4, bit(2) == 1)
                stats = cr[h, 1]
                five = (cr[h, 0], jnp.broadcast_to(stats[:, :1], (32, HEAD)),
                        jnp.broadcast_to(stats[:, 64:65], (32, HEAD)))
                state = merge(widen(five, w, 2), four)
                state = merge(widen(state, w, 2), three)
                state = widen(state, w, 8)
                num, _, total = merge(tuple(base[h, i] for i in range(3)), state)
                outb[hp, :, cols] = (num / total).astype(BF)
            out_copy(hp).start()
        return 0

    lax.fori_loop(0, PAIRS + 1, final_pair, 0)

    def drain(hp, _):
        out_copy(hp).wait()

        @pl.when(core == 0)
        def _():
            send2(hp).wait_send()

        @pl.when(bit(1) == 0)
        def _():
            send3(hp).wait_send()

        @pl.when(bit(1) == 1)
        def _():
            relay3(hp).wait_send()

        @pl.when(bit(2) == 0)
        def _():
            send4(hp, 0).wait_send()
            send4(hp, 1).wait_send()

        @pl.when(bit(2) == 1)
        def _():
            relay4(hp).wait_send()
        return 0

    lax.fori_loop(0, PAIRS, drain, 0)

    def drain_octet(h, _):
        @pl.when(h != own)
        def _():
            send_a(h).wait_send()
            send_c(h).wait_send()
        return 0

    lax.fori_loop(0, 8, drain_octet, 0)
    for level in range(8, 4, -1):
        n = 1 << (level - 5)

        @pl.when(bit(level - 2) == 0)
        def _():
            for i in range(n):
                copy_b(level, i).wait_send()


def attend(queries, keys, values):
    count, width = queries.shape
    vm = lambda *shape: pltpu.VMEM(shape, BF)
    vf = lambda *shape: pltpu.VMEM(shape, F32)
    dma = lambda *shape: pltpu.SemaphoreType.DMA(shape)
    scratch = [
        vm(4, 1024, 256), vm(4, 1024, 256), vm(4, 1024, 256),
        vm(4, 304, 256), vf(256, 256),
        vm(4, 2, 256, 256), vm(4, 256, 256),
        vm(4, 2, 256, 256), vm(4, 256, 256), vm(4, 2, 256, 256),
        vm(4, 2, 128, 256), vm(4, 128, 256), vm(4, 2, 2, 128, 256),
        vm(4, 2, 64, 256), vm(4, 64, 256), vm(4, 2, 2, 2, 64, 256),
        vm(8, 2, 64, 128), vm(8, 2, 64, 128), vm(2, 512, 128),
        vm(1, 2, 256, 128), vm(2, 2, 128, 128), vm(4, 2, 64, 128), vm(8, 2, 32, 128),
        vf(8, 2, 32, 128), vf(8, 2, 32, 128),
        vf(2, 3, 1024, 128), vf(8, 3, 1024, 128), vm(4, 1024, 256),
        dma(4, 3), dma(4),
        dma(4), dma(4),
        dma(4), dma(4), dma(4), dma(4),
        dma(4, 2), dma(4, 2), dma(4), dma(4),
        dma(8), dma(8), dma(15), dma(15), dma(8), dma(8),
    ]
    return pl.pallas_call(
        kernel,
        out_shape=jax.ShapeDtypeStruct((count, width), BF),
        in_specs=[pl.BlockSpec(memory_space=pl.ANY)] * 3,
        out_specs=pl.BlockSpec(memory_space=pl.ANY),
        scratch_shapes=scratch,
        compiler_params=pltpu.CompilerParams(
            collective_id=0, has_side_effects=True, vmem_limit_bytes=56 * 1024 * 1024
        ),
        name="hierarchical_attention",
    )(queries, keys, values)


def on_device(queries, keys, values, w_out):
    attended = attend(queries, keys, values)
    return jnp.dot(attended, w_out, preferred_element_type=F32).astype(BF)


def solution(mesh):
    return jax.shard_map(
        on_device,
        mesh=mesh,
        in_specs=(P("seq", None), P("seq", None), P("seq", None), P()),
        out_specs=P("seq", None),
        check_vma=False,
    )
```

```python
import functools
import math

import jax
import jax.numpy as jnp
from jax import lax
from jax.experimental import pallas as pl
from jax.experimental.pallas import tpu as pltpu
from jax.sharding import PartitionSpec as P

MESH = pl.DeviceIdType.MESH
HEAD = 128
PAIRS = 4
WIDE = 256
NEG = -1e30
C2 = HEAD ** -0.5 * math.log2(math.e)
BF = jnp.bfloat16
F32 = jnp.float32


def nt_dot(a, b):
    return lax.dot_general(a, b, (((1,), (1,)), ((), ())), preferred_element_type=F32)


def dot(a, b):
    return lax.dot_general(a, b, (((1,), (0,)), ((), ())), preferred_element_type=F32)


def tile_scores(tile):
    q, keys = tile["q"](), tile["k"]()
    scores = [nt_dot(q, k) for k in keys]
    if tile["bias"] is not None:
        scores[-1] = scores[-1] + tile["bias"][...]
    return scores


def tile_probs(tile, scores):
    scale = C2 * 4.0 ** -tile["level"]
    peak = None
    for s in scores:
        top = jnp.max(s, axis=1, keepdims=True)
        peak = top if peak is None else jnp.maximum(peak, top)
    probs, total = [], None
    for s in scores:
        p = jnp.exp2((s - peak) * scale)
        row = jnp.sum(p, axis=1, keepdims=True)
        total = row if total is None else total + row
        probs.append(p.astype(BF))
    return probs, peak, total


def tile_out(tile, probs, peak, total):
    num = None
    for p, v in zip(probs, tile["v"]()):
        part = dot(p, v)
        num = part if num is None else num + part
    tile["sink"](num, peak, total)


def run_tiles(tiles):
    scores, probs = {}, {}
    count = len(tiles)
    for i in range(count + 2):
        if i < count:
            scores[i] = tile_scores(tiles[i])
        if 1 <= i <= count:
            probs[i - 1] = tile_probs(tiles[i - 1], scores.pop(i - 1))
        if i >= 2:
            tile_out(tiles[i - 2], *probs.pop(i - 2))


def coarse_tile(level, q, k, v, flag, sink):
    def done(num, peak, total):
        peak = jnp.broadcast_to(peak * 4.0 ** -level, num.shape)
        total = jnp.broadcast_to(total * 2.0 ** level, num.shape)
        if flag is not None:
            num = jnp.where(flag, num, 0.0)
            peak = jnp.where(flag, peak, NEG)
            total = jnp.where(flag, total, 0.0)
        sink(num, peak, total)
    return {"q": q, "k": lambda: [k()], "v": lambda: [v()], "bias": None, "level": level, "sink": done}


def store(ref, *index):
    def sink(*planes):
        for i, plane in enumerate(planes):
            ref[(*index, i)] = plane
    return sink


def merge(a, b):
    top = jnp.maximum(a[1], b[1])
    fa = jnp.exp2((a[1] - top) * C2)
    fb = jnp.exp2((b[1] - top) * C2)
    return fa * a[0] + fb * b[0], top, fa * a[2] + fb * b[2]


def widen(state, ref, times, start=0):
    rows = state[0].shape[0]
    for plane, value in enumerate(state):
        for r in range(times):
            ref[plane, pl.ds(start + r, rows, stride=times), :] = value
    return tuple(ref[i, pl.ds(start, rows * times), :] for i in range(len(state)))


def kernel(q_hbm, k_hbm, v_hbm, att_hbm, qb, kb, vb, pool, bias,
           kv1, q1, kv2, q2, r2, kv3, q3, r3, kv4, q4, r4, f4,
           ts, rt, xs, r5, r6, r7, r8, cs, cr, wide, base, near, far, deep, outb,
           load_sem, out_sem, s2, g2, s3, g3, y3, z3, s4, g4, h4, y4, z4,
           sa, ga, sb, gb, sc, gc):
    me = lax.axis_index("seq")
    core = me & 1
    own = me & 7
    octet = me - own

    def bit(i):
        return (me >> i) & 1

    def load(hp, t):
        src = (k_hbm, v_hbm, q_hbm)[t]
        dst = (kb, vb, qb)[t]
        cols = pl.ds(pl.multiple_of(hp * WIDE, WIDE), WIDE)
        return pltpu.make_async_copy(src.at[:, cols], dst.at[hp], load_sem.at[hp, t])

    for hp in range(PAIRS):
        for t in range(3):
            load(hp, t).start()

    barrier = pltpu.get_barrier_semaphore()
    masks = list(range(1, 8)) + [8 * o for o in range(1, 16)]

    def greet(i, _):
        mask = jnp.where(i < 8, i, (i - 7) * 8)
        pl.semaphore_signal(barrier, inc=1, device_id=(me ^ mask,), device_id_type=MESH)
        return 0

    lax.fori_loop(1, 23, greet, 0)

    row = lax.broadcasted_iota(jnp.int32, (304, WIDE), 0)
    col = lax.broadcasted_iota(jnp.int32, (304, WIDE), 1)
    tail = row >= 240
    shift = jnp.where(row < 128, 1, jnp.where(row < 192, 2, jnp.where(row < 224, 3, 4)))
    off = jnp.where(row < 128, row, jnp.where(row < 192, row - 128, jnp.where(row < 224, row - 192, row - 224)))
    t = row - 240
    shift_t = jnp.where(t < 32, 5, jnp.where(t < 48, 6, jnp.where(t < 56, 7, 8)))
    off_t = jnp.where(t < 32, t, jnp.where(t < 48, t - 32, jnp.where(t < 56, t - 48, t - 56)))
    shift = jnp.where(tail, shift_t, shift)
    off = jnp.where(tail, off_t, off)
    for i in range(4):
        at = jnp.where(tail, col + 256 * i, col)
        pool[i] = jnp.where((at >> shift) == off, 1.0, 0.0).astype(BF)
    r_i = lax.broadcasted_iota(jnp.int32, (256, 256), 0)
    c_i = lax.broadcasted_iota(jnp.int32, (256, 256), 1)
    bias[...] = jnp.where(c_i <= r_i, 0.0, NEG)

    tr = lax.broadcasted_iota(jnp.int32, (64, WIDE), 0)
    side = jnp.where(tr < 32, bit(3), jnp.where(tr < 48, bit(4), jnp.where(tr < 56, bit(5), bit(6))))

    def copy_to(src, dst, send, recv, device):
        return pltpu.make_async_remote_copy(src_ref=src, dst_ref=dst, send_sem=send, recv_sem=recv,
                                            device_id=(device,), device_id_type=MESH)

    def send2(hp):
        return copy_to(kv2.at[hp], r2.at[hp], s2.at[hp], g2.at[hp], me ^ 1)

    def send3(hp):
        return copy_to(kv3.at[hp], r3.at[hp, core], s3.at[hp], g3.at[hp], me ^ 2)

    def relay3(hp):
        return copy_to(r3.at[hp, core], r3.at[hp, core], y3.at[hp], z3.at[hp], me ^ 1)

    def send4(hp):
        return copy_to(kv4.at[hp], r4.at[hp, core, bit(1)], s4.at[hp, 0], g4.at[hp, 0], me ^ 6)

    def recv4(hp, j):
        return copy_to(kv4.at[hp], r4.at[hp, core, bit(1) ^ 1 ^ j], s4.at[hp, j], g4.at[hp, j], me ^ 6)

    def lend4(hp):
        return copy_to(kv4.at[hp], f4.at[hp], s4.at[hp, 1], h4.at[hp], me ^ 2)

    def pass4(hp):
        return copy_to(f4.at[hp], r4.at[hp, core, 1], s4.at[hp, 1], g4.at[hp, 1], me ^ 6)

    def hand4(hp):
        return copy_to(r4.at[hp, core, 0], r4.at[hp, core, 0], s4.at[hp, 0], g4.at[hp, 1], me ^ 2)

    def forward4(hp):
        @pl.when(own < 2)
        def _():
            lend4(hp).wait_recv()
            pass4(hp).start()

        @pl.when(own >= 6)
        def _():
            recv4(hp, 0).wait_recv()
            hand4(hp).start()

    def relay4(hp):
        return copy_to(r4.at[hp, core], r4.at[hp, core], y4.at[hp], z4.at[hp], me ^ 1)

    def send_a(h):
        return copy_to(ts.at[h], rt.at[own], sa.at[h], ga.at[own], octet + h)

    def recv_a(h):
        return copy_to(ts.at[h], rt.at[h], sa.at[h], ga.at[h], octet + h)

    def send_c(h):
        return copy_to(cs.at[h], cr.at[own], sc.at[h], gc.at[own], octet + h)

    def recv_c(h):
        return copy_to(cs.at[h], cr.at[h], sc.at[h], gc.at[h], octet + h)

    def copy_b(level, i):
        count = 256 >> (level - 5)
        start = (0, 256, 384, 448)[level - 5]
        n = 1 << (level - 5)
        dst = (r5, r6, r7, r8)[level - 5]
        slot = n - 1 + i
        mask = 8 * (n + i)
        return copy_to(xs.at[:, pl.ds(start, count)], dst.at[i], sb.at[slot], gb.at[slot], me ^ mask)

    def pool_pair(hp, _):
        tails = []
        for t in range(3):
            load(hp, t).wait()
            src = (kb, vb, qb)[t]
            acc = None
            ys = {}
            for step in range(5):
                if step < 4:
                    start = 0 if (step < 2) == (t < 2) else 128
                    ys[step] = (start, dot(pool[step, start:], src[hp, step * 256:(step + 1) * 256, :]))
                if step == 0:
                    continue
                i = step - 1
                start, y = ys.pop(i)
                yb = y[:240 - start].astype(BF)
                mid = 128 - start
                if start == 0:
                    if t < 2:
                        kv1[hp, t, i * 128:(i + 1) * 128, :] = yb[:128]
                    else:
                        q1[hp, (i - 2) * 128:(i - 1) * 128, :] = yb[:128]
                if t < 2:
                    kv2[hp, t, i * 64:(i + 1) * 64, :] = yb[mid:mid + 64]
                    kv3[hp, t, i * 32:(i + 1) * 32, :] = yb[mid + 64:mid + 96]
                    kv4[hp, t, i * 16:(i + 1) * 16, :] = yb[mid + 96:mid + 112]
                else:
                    q2[hp, i * 64:(i + 1) * 64, :] = yb[mid:mid + 64]
                    q3[hp, i * 32:(i + 1) * 32, :] = yb[mid + 64:mid + 96]
                    q4[hp, i * 16:(i + 1) * 16, :] = yb[mid + 96:mid + 112]
                acc = y[mid + 112:] if acc is None else acc + y[mid + 112:]
            tails.append(acc)

        @pl.when(hp == 0)
        def _():
            pl.semaphore_wait(barrier, len(masks))

        first = jnp.where(side == 0, tails[0], tails[2]).astype(BF)
        second = tails[1].astype(BF)
        for e in range(2):
            h = 2 * hp + e
            ts[h, 0] = first[:, e * HEAD:(e + 1) * HEAD]
            ts[h, 1] = second[:, e * HEAD:(e + 1) * HEAD]

            @pl.when(h != own)
            def _():
                send_a(h).start()

        return 0

    lax.fori_loop(0, PAIRS, pool_pair, 0)

    def near4(hp, _):
        @pl.when(bit(2) == 0)
        def _():
            send4(hp).start()

        @pl.when((own & 6) == 2)
        def _():
            lend4(hp).start()

        return 0

    def near3(hp, _):
        @pl.when(bit(1) == 0)
        def _():
            send3(hp).start()

        return 0

    def near2(hp, _):
        @pl.when(core == 0)
        def _():
            send2(hp).start()

        return 0

    lax.fori_loop(0, PAIRS, near2, 0)
    lax.fori_loop(0, PAIRS, near4, 0)
    lax.fori_loop(0, 4, near3, 0)
    rt[own] = ts[own]

    def wait_a():
        def one(h, _):
            @pl.when(h != own)
            def _():
                recv_a(h).wait_recv()
            return 0
        lax.fori_loop(0, 8, one, 0)
        i = lax.broadcasted_iota(jnp.int32, (512, 512), 0)
        j = lax.broadcasted_iota(jnp.int32, (512, 512), 1)
        i6, i7, i8 = i - 256, i - 384, i - 448
        at = jnp.where(i < 256, (i >> 5) * 64 + (i & 31),
             jnp.where(i < 384, (i6 >> 4) * 64 + 32 + (i6 & 15),
             jnp.where(i < 448, (i7 >> 3) * 64 + 48 + (i7 & 7),
             jnp.where(i < 480, (i8 >> 2) * 64 + 56 + (i8 & 3), -1))))
        move = jnp.where(at == j, 1.0, 0.0).astype(BF)
        both = jnp.concatenate([rt[:, 0].reshape(512, HEAD), rt[:, 1].reshape(512, HEAD)], axis=1)
        x = dot(move, both).astype(BF)
        xs[0] = x[:, :HEAD]
        xs[1] = x[:, HEAD:]
        for level in range(8, 4, -1):
            n = 1 << (level - 5)

            @pl.when(bit(level - 2) == 0)
            def _():
                for i in range(n):
                    copy_b(level, i).start()

    def wait_b():
        for level in range(8, 4, -1):
            n = 1 << (level - 5)

            @pl.when(bit(level - 2) == 1)
            def _():
                for i in range(n):
                    copy_b(level, i).wait_recv()
        tiles = []
        for level, ref in ((8, r8), (7, r7), (6, r6), (5, r5)):
            start = (0, 256, 384, 448)[level - 5]
            rows = 256 >> (level - 5)
            tiles.append(coarse_tile(
                level, lambda start=start, rows=rows: xs[0, start:start + rows, :],
                lambda ref=ref: ref[:, 0].reshape(256, HEAD), lambda ref=ref: ref[:, 1].reshape(256, HEAD),
                bit(level - 2) == 1, lambda *x, start=start, rows=rows: deep.__setitem__(
                    (slice(None), slice(start, start + rows)), jnp.stack(x))))
        run_tiles(tiles)
        deep_of = lambda start, rows: tuple(deep[i, start:start + rows, :] for i in range(3))
        state = deep_of(448, 32)
        for start, rows in ((384, 64), (256, 128), (0, 256)):
            state = merge(widen(state, wide.at[0], 2), deep_of(start, rows))
        lane = lax.broadcasted_iota(jnp.int32, (256, HEAD), 1)
        place = lax.broadcasted_iota(jnp.int32, (256, HEAD), 0) & 31
        stats = jnp.where(lane == place, state[1], jnp.where(lane == place + 32, state[2], 0.0))
        stats = jnp.sum(stats.reshape(8, 32, HEAD), axis=1, keepdims=True)
        cs[:, :32] = state[0].reshape(8, 32, HEAD)
        cs[:, 32:] = jnp.broadcast_to(stats, (8, 8, HEAD))
        cr[own] = cs[own]

        def one(h, _):
            @pl.when(h != own)
            def _():
                send_c(h).start()
            return 0
        lax.fori_loop(0, 8, one, 0)

    def local_pair(hp, _):
        @pl.when(core == 1)
        def _():
            send2(hp).wait_recv()
        tiles = []
        for e in range(2):
            cols = slice(e * HEAD, (e + 1) * HEAD)
            h = 2 * hp + e
            for seg in range(2):
                for half in range(2):
                    at, begin = seg * 512 + half * 256, seg * 512

                    def sink(num, peak, total, at=at, h=h):
                        base[h, 0, at:at + 256, :] = num * (1.0 / total)
                        lse = peak + jnp.log2(total) * (1.0 / C2)
                        base[h, 1, at:at + 256, :] = jnp.broadcast_to(lse, num.shape)

                    def parts(ref, begin=begin, half=half, cols=cols):
                        return [ref[hp, begin + i * 256:begin + (i + 1) * 256, cols] for i in range(half + 1)]

                    tiles.append({"q": lambda at=at, cols=cols: qb[hp, at:at + 256, cols],
                                  "k": lambda parts=parts: parts(kb), "v": lambda parts=parts: parts(vb),
                                  "bias": bias, "level": 0, "sink": sink})
            tiles.append(coarse_tile(1, lambda cols=cols: q1[hp, :, cols], lambda cols=cols: kv1[hp, 0, :, cols],
                                     lambda cols=cols: kv1[hp, 1, :, cols], None, store(near, h)))
            tiles.append(coarse_tile(2, lambda cols=cols: q2[hp, :, cols], lambda cols=cols: r2[hp, 0, :, cols],
                                     lambda cols=cols: r2[hp, 1, :, cols], core == 1, store(far, h)))
        run_tiles(tiles)
        forward4(hp)

        @pl.when(hp == 0)
        def _():
            wait_a()

        @pl.when(hp == 2)
        def _():
            wait_b()
        return 0

    lax.fori_loop(0, PAIRS, local_pair, 0)

    def recv_c_all(h, _):
        @pl.when(h != own)
        def _():
            recv_c(h).wait_recv()
        return 0

    lax.fori_loop(0, 8, recv_c_all, 0)

    def out_copy(hp):
        cols = pl.ds(pl.multiple_of(hp * WIDE, WIDE), WIDE)
        return pltpu.make_async_copy(outb.at[hp], att_hbm.at[:, cols], out_sem.at[hp])

    def final_pair(step, _):
        @pl.when(step < PAIRS)
        def _():
            @pl.when(bit(2) == 1)
            def _():
                @pl.when(bit(1) == 0)
                def _():
                    recv4(step, 0).wait_recv()
                recv4(step, 1).wait_recv()
                relay4(step).start()

            @pl.when(bit(1) == 1)
            def _():
                send3(step).wait_recv()
                relay3(step).start()

        @pl.when(step > 0)
        def _():
            hp = step - 1

            @pl.when(bit(2) == 1)
            def _():
                copy_to(r4.at[hp, 1 - core], r4.at[hp, 1 - core], y4.at[hp], z4.at[hp], me ^ 1).wait_recv()

            @pl.when(bit(1) == 1)
            def _():
                copy_to(r3.at[hp, 1 - core], r3.at[hp, 1 - core], y3.at[hp], z3.at[hp], me ^ 1).wait_recv()

            tiles, threes, fours = [], [None] * 2, [None] * 2

            def keep(into, e):
                return lambda *x: into.__setitem__(e, x)

            for e in range(2):
                cols = slice(e * HEAD, (e + 1) * HEAD)
                tiles.append(coarse_tile(
                    4, lambda cols=cols: q4[hp, :, cols],
                    lambda cols=cols: r4[hp, :, :, 0, :, cols].reshape(256, HEAD),
                    lambda cols=cols: r4[hp, :, :, 1, :, cols].reshape(256, HEAD), bit(2) == 1, keep(fours, e)))
                tiles.append(coarse_tile(
                    3, lambda cols=cols: q3[hp, :, cols],
                    lambda cols=cols: r3[hp, :, 0, :, cols].reshape(256, HEAD),
                    lambda cols=cols: r3[hp, :, 1, :, cols].reshape(256, HEAD), bit(1) == 1, keep(threes, e)))
            run_tiles(tiles)
            r32 = lax.broadcasted_iota(jnp.int32, (32, HEAD), 0)
            l32 = lax.broadcasted_iota(jnp.int32, (32, HEAD), 1)
            states = []
            for e in range(2):
                h = 2 * hp + e
                stats = jnp.broadcast_to(cr[h, 32:33, :], (32, HEAD))
                column = lambda at: jnp.broadcast_to(
                    jnp.sum(jnp.where(l32 == at, stats, 0.0), axis=1, keepdims=True), (32, HEAD))
                states.append((cr[h, :32, :], column(r32), column(r32 + 32)))
            for terms in (fours, threes, None):
                for e in range(2):
                    term = terms[e] if terms is not None else tuple(far[2 * hp + e, i] for i in range(3))
                    states[e] = merge(widen(states[e], wide.at[e], 2), term)
            for e in range(2):
                h = 2 * hp + e
                low = tuple(x[:128] for x in states[e])
                high = tuple(x[128:] for x in states[e])
                high = merge(widen(high, wide.at[e], 2, 512), tuple(near[h, i] for i in range(3)))
                for (num, peak, total), times, at in ((low, 4, 0), (high, 2, 512)):
                    seen = total > 0.0
                    safe = jnp.where(seen, total, 1.0)
                    pair = (num * (1.0 / safe), jnp.where(seen, peak + jnp.log2(safe) * (1.0 / C2), NEG))
                    coarse, lse = widen(pair, wide.at[e], times, at)
                    fine, fine_lse = base[h, 0, at:at + 512, :], base[h, 1, at:at + 512, :]
                    share = 1.0 / (1.0 + jnp.exp2((fine_lse - lse) * C2))
                    outb[hp, at:at + 512, e * HEAD:(e + 1) * HEAD] = (fine + share * (coarse - fine)).astype(BF)
            out_copy(hp).start()
        return 0

    lax.fori_loop(0, PAIRS + 1, final_pair, 0)

    def drain(hp, _):
        out_copy(hp).wait()

        @pl.when(core == 0)
        def _():
            send2(hp).wait_send()

        @pl.when(bit(1) == 0)
        def _():
            send3(hp).wait_send()

        @pl.when(bit(1) == 1)
        def _():
            relay3(hp).wait_send()

        @pl.when(bit(2) == 0)
        def _():
            send4(hp).wait_send()
            lend4(hp).wait_send()

        @pl.when(bit(2) == 1)
        def _():
            relay4(hp).wait_send()

        @pl.when(own >= 6)
        def _():
            hand4(hp).wait_send()
        return 0

    lax.fori_loop(0, PAIRS, drain, 0)

    def drain_octet(h, _):
        @pl.when(h != own)
        def _():
            send_a(h).wait_send()
            send_c(h).wait_send()
        return 0

    lax.fori_loop(0, 8, drain_octet, 0)
    for level in range(8, 4, -1):
        n = 1 << (level - 5)

        @pl.when(bit(level - 2) == 0)
        def _():
            for i in range(n):
                copy_b(level, i).wait_send()


def attend(queries, keys, values):
    count, width = queries.shape
    vm = lambda *shape: pltpu.VMEM(shape, BF)
    vf = lambda *shape: pltpu.VMEM(shape, F32)
    dma = lambda *shape: pltpu.SemaphoreType.DMA(shape)
    scratch = [
        vm(4, 1024, 256), vm(4, 1024, 256), vm(4, 1024, 256),
        vm(4, 304, 256), vf(256, 256),
        vm(4, 2, 256, 256), vm(4, 256, 256),
        vm(4, 2, 256, 256), vm(4, 256, 256), vm(4, 2, 256, 256),
        vm(4, 2, 128, 256), vm(4, 128, 256), vm(4, 2, 2, 128, 256),
        vm(4, 2, 64, 256), vm(4, 64, 256), vm(4, 2, 2, 2, 64, 256), vm(4, 2, 64, 256),
        vm(8, 2, 64, 128), vm(8, 2, 64, 128), vm(2, 512, 128),
        vm(1, 2, 256, 128), vm(2, 2, 128, 128), vm(4, 2, 64, 128), vm(8, 2, 32, 128),
        vf(8, 40, 128), vf(8, 40, 128),
        vf(2, 3, 1024, 128), vf(8, 2, 1024, 128),
        vf(8, 3, 256, 128), vf(8, 3, 256, 128), vf(3, 480, 128), vm(4, 1024, 256),
        dma(4, 3), dma(4),
        dma(4), dma(4),
        dma(4), dma(4), dma(4), dma(4),
        dma(4, 2), dma(4, 2), dma(4), dma(4), dma(4),
        dma(8), dma(8), dma(15), dma(15), dma(8), dma(8),
    ]
    return pl.pallas_call(
        kernel,
        out_shape=jax.ShapeDtypeStruct((count, width), BF),
        in_specs=[pl.BlockSpec(memory_space=pl.ANY)] * 3,
        out_specs=pl.BlockSpec(memory_space=pl.ANY),
        scratch_shapes=scratch,
        compiler_params=pltpu.CompilerParams(
            collective_id=0, has_side_effects=True, vmem_limit_bytes=56 * 1024 * 1024
        ),
        name="hierarchical_attention",
    )(queries, keys, values)


def on_device(queries, keys, values, w_out):
    attended = attend(queries, keys, values)
    return jnp.dot(attended, w_out, preferred_element_type=F32).astype(BF)


def solution(mesh):
    return jax.shard_map(
        on_device,
        mesh=mesh,
        in_specs=(P("seq", None), P("seq", None), P("seq", None), P()),
        out_specs=P("seq", None),
        check_vma=False,
    )
```

```python
import functools
import math

import jax
import jax.numpy as jnp
from jax import lax
from jax.experimental import pallas as pl
from jax.experimental.pallas import tpu as pltpu
from jax.sharding import PartitionSpec as P

MESH = pl.DeviceIdType.MESH
HEAD = 128
PAIRS = 4
WIDE = 256
NEG = -1e30
C2 = HEAD ** -0.5 * math.log2(math.e)
BF = jnp.bfloat16
F32 = jnp.float32


def nt_dot(a, b):
    return lax.dot_general(a, b, (((1,), (1,)), ((), ())), preferred_element_type=F32)


def dot(a, b):
    return lax.dot_general(a, b, (((1,), (0,)), ((), ())), preferred_element_type=F32)


def tile_scores(tile):
    q, keys = tile["q"](), tile["k"]()
    scores = [nt_dot(q, k) for k in keys]
    if tile["bias"] is not None:
        scores[-1] = scores[-1] + tile["bias"][...]
    return scores


def tile_probs(tile, scores):
    scale = C2 * 4.0 ** -tile["level"]
    peak = None
    for s in scores:
        top = jnp.max(s, axis=1, keepdims=True)
        peak = top if peak is None else jnp.maximum(peak, top)
    probs, total = [], None
    for s in scores:
        p = jnp.exp2((s - peak) * scale)
        row = jnp.sum(p, axis=1, keepdims=True)
        total = row if total is None else total + row
        probs.append(p.astype(BF))
    return probs, peak, total


def tile_out(tile, probs, peak, total):
    num = None
    for p, v in zip(probs, tile["v"]()):
        part = dot(p, v)
        num = part if num is None else num + part
    tile["sink"](num, peak, total)


def run_tiles(tiles):
    scores, probs = {}, {}
    count = len(tiles)
    for i in range(count + 2):
        if i < count:
            scores[i] = tile_scores(tiles[i])
        if 1 <= i <= count:
            probs[i - 1] = tile_probs(tiles[i - 1], scores.pop(i - 1))
        if i >= 2:
            tile_out(tiles[i - 2], *probs.pop(i - 2))


def coarse_tile(level, q, k, v, flag, sink):
    def done(num, peak, total):
        peak = jnp.broadcast_to(peak * 4.0 ** -level, num.shape)
        total = jnp.broadcast_to(total * 2.0 ** level, num.shape)
        if flag is not None:
            num = jnp.where(flag, num, 0.0)
            peak = jnp.where(flag, peak, NEG)
            total = jnp.where(flag, total, 0.0)
        sink(num, peak, total)
    return {"q": q, "k": lambda: [k()], "v": lambda: [v()], "bias": None, "level": level, "sink": done}


def store(ref, *index):
    def sink(*planes):
        for i, plane in enumerate(planes):
            ref[(*index, i)] = plane
    return sink


def merge(a, b):
    top = jnp.maximum(a[1], b[1])
    fa = jnp.exp2((a[1] - top) * C2)
    fb = jnp.exp2((b[1] - top) * C2)
    return fa * a[0] + fb * b[0], top, fa * a[2] + fb * b[2]


def widen(state, ref, times, start=0):
    rows = state[0].shape[0]
    for plane, value in enumerate(state):
        for r in range(times):
            ref[plane, pl.ds(start + r, rows, stride=times), :] = value
    return tuple(ref[i, pl.ds(start, rows * times), :] for i in range(len(state)))


def kernel(q_hbm, k_hbm, v_hbm, att_hbm, qb, kb, vb, pool, bias,
           kv1, q1, kv2, q2, r2, kv3, q3, r3, kv4, q4, r4, f4,
           ts, rt, xs, r5, r6, r7, r8, cs, cr, wide, base, near, far, deep, outb,
           load_sem, out_sem, s2, g2, s3, g3, y3, z3, s4, g4, h4, y4, z4,
           sa, ga, sb, gb, sc, gc):
    me = lax.axis_index("seq")
    core = me & 1
    own = me & 7
    octet = me - own

    def bit(i):
        return (me >> i) & 1

    def load(hp, t):
        src = (k_hbm, v_hbm, q_hbm)[t]
        dst = (kb, vb, qb)[t]
        cols = pl.ds(pl.multiple_of(hp * WIDE, WIDE), WIDE)
        return pltpu.make_async_copy(src.at[:, cols], dst.at[hp], load_sem.at[hp, t])

    for hp in range(PAIRS):
        for t in range(3):
            load(hp, t).start()

    barrier = pltpu.get_barrier_semaphore()
    masks = list(range(1, 8)) + [8 * o for o in range(1, 16)]

    def greet(i, _):
        mask = jnp.where(i < 8, i, (i - 7) * 8)
        pl.semaphore_signal(barrier, inc=1, device_id=(me ^ mask,), device_id_type=MESH)
        return 0

    lax.fori_loop(1, 23, greet, 0)

    row = lax.broadcasted_iota(jnp.int32, (304, WIDE), 0)
    col = lax.broadcasted_iota(jnp.int32, (304, WIDE), 1)
    tail = row >= 240
    shift = jnp.where(row < 128, 1, jnp.where(row < 192, 2, jnp.where(row < 224, 3, 4)))
    off = jnp.where(row < 128, row, jnp.where(row < 192, row - 128, jnp.where(row < 224, row - 192, row - 224)))
    t = row - 240
    shift_t = jnp.where(t < 32, 5, jnp.where(t < 48, 6, jnp.where(t < 56, 7, 8)))
    off_t = jnp.where(t < 32, t, jnp.where(t < 48, t - 32, jnp.where(t < 56, t - 48, t - 56)))
    shift = jnp.where(tail, shift_t, shift)
    off = jnp.where(tail, off_t, off)
    for i in range(4):
        at = jnp.where(tail, col + 256 * i, col)
        pool[i] = jnp.where((at >> shift) == off, 1.0, 0.0).astype(BF)
    r_i = lax.broadcasted_iota(jnp.int32, (256, 256), 0)
    c_i = lax.broadcasted_iota(jnp.int32, (256, 256), 1)
    bias[...] = jnp.where(c_i <= r_i, 0.0, NEG)

    tr = lax.broadcasted_iota(jnp.int32, (64, WIDE), 0)
    side = jnp.where(tr < 32, bit(3), jnp.where(tr < 48, bit(4), jnp.where(tr < 56, bit(5), bit(6))))

    def copy_to(src, dst, send, recv, device):
        return pltpu.make_async_remote_copy(src_ref=src, dst_ref=dst, send_sem=send, recv_sem=recv,
                                            device_id=(device,), device_id_type=MESH)

    def send2(hp):
        return copy_to(kv2.at[hp], r2.at[hp], s2.at[hp], g2.at[hp], me ^ 1)

    def send3(hp):
        return copy_to(kv3.at[hp], r3.at[hp, core], s3.at[hp], g3.at[hp], me ^ 2)

    def relay3(hp):
        return copy_to(r3.at[hp, core], r3.at[hp, core], y3.at[hp], z3.at[hp], me ^ 1)

    def send4(hp):
        return copy_to(kv4.at[hp], r4.at[hp, core, bit(1)], s4.at[hp, 0], g4.at[hp, 0], me ^ 6)

    def recv4(hp, j):
        return copy_to(kv4.at[hp], r4.at[hp, core, bit(1) ^ 1 ^ j], s4.at[hp, j], g4.at[hp, j], me ^ 6)

    def lend4(hp):
        return copy_to(kv4.at[hp], f4.at[hp], s4.at[hp, 1], h4.at[hp], me ^ 2)

    def pass4(hp):
        return copy_to(f4.at[hp], r4.at[hp, core, 1], s4.at[hp, 1], g4.at[hp, 1], me ^ 6)

    def hand4(hp):
        return copy_to(r4.at[hp, core, 0], r4.at[hp, core, 0], s4.at[hp, 0], g4.at[hp, 1], me ^ 2)

    def forward4(hp):
        @pl.when(own < 2)
        def _():
            lend4(hp).wait_recv()
            pass4(hp).start()

        @pl.when(own >= 6)
        def _():
            recv4(hp, 0).wait_recv()
            hand4(hp).start()

    def relay4(hp):
        return copy_to(r4.at[hp, core], r4.at[hp, core], y4.at[hp], z4.at[hp], me ^ 1)

    def send_a(h):
        return copy_to(ts.at[h], rt.at[own], sa.at[h], ga.at[own], octet + h)

    def recv_a(h):
        return copy_to(ts.at[h], rt.at[h], sa.at[h], ga.at[h], octet + h)

    def send_c(h):
        return copy_to(cs.at[h], cr.at[own], sc.at[h], gc.at[own], octet + h)

    def recv_c(h):
        return copy_to(cs.at[h], cr.at[h], sc.at[h], gc.at[h], octet + h)

    def copy_b(level, i):
        count = 256 >> (level - 5)
        start = (0, 256, 384, 448)[level - 5]
        n = 1 << (level - 5)
        dst = (r5, r6, r7, r8)[level - 5]
        slot = n - 1 + i
        mask = 8 * (n + i)
        return copy_to(xs.at[:, pl.ds(start, count)], dst.at[i], sb.at[slot], gb.at[slot], me ^ mask)

    def pool_pair(hp, _):
        tails = []
        for t in range(3):
            load(hp, t).wait()
            src = (kb, vb, qb)[t]
            acc = None
            ys = {}
            for step in range(5):
                if step < 4:
                    start = 0 if (step < 2) == (t < 2) else 128
                    ys[step] = (start, dot(pool[step, start:], src[hp, step * 256:(step + 1) * 256, :]))
                if step == 0:
                    continue
                i = step - 1
                start, y = ys.pop(i)
                yb = y[:240 - start].astype(BF)
                mid = 128 - start
                if start == 0:
                    if t < 2:
                        kv1[hp, t, i * 128:(i + 1) * 128, :] = yb[:128]
                    else:
                        q1[hp, (i - 2) * 128:(i - 1) * 128, :] = yb[:128]
                if t < 2:
                    kv2[hp, t, i * 64:(i + 1) * 64, :] = yb[mid:mid + 64]
                    kv3[hp, t, i * 32:(i + 1) * 32, :] = yb[mid + 64:mid + 96]
                    kv4[hp, t, i * 16:(i + 1) * 16, :] = yb[mid + 96:mid + 112]
                else:
                    q2[hp, i * 64:(i + 1) * 64, :] = yb[mid:mid + 64]
                    q3[hp, i * 32:(i + 1) * 32, :] = yb[mid + 64:mid + 96]
                    q4[hp, i * 16:(i + 1) * 16, :] = yb[mid + 96:mid + 112]
                acc = y[mid + 112:] if acc is None else acc + y[mid + 112:]
            tails.append(acc)

        first = jnp.where(side == 0, tails[0], tails[2]).astype(BF)
        second = tails[1].astype(BF)
        for e in range(2):
            h = 2 * hp + e
            ts[h, 0] = first[:, e * HEAD:(e + 1) * HEAD]
            ts[h, 1] = second[:, e * HEAD:(e + 1) * HEAD]

        return 0

    lax.fori_loop(0, PAIRS, pool_pair, 0)
    pl.semaphore_wait(barrier, len(masks))

    def octet_sends(i, _):
        send_a((own + i) & 7).start()
        return 0

    lax.fori_loop(1, 8, octet_sends, 0)

    def near4(hp, _):
        @pl.when(bit(2) == 0)
        def _():
            send4(hp).start()

        @pl.when((own & 6) == 2)
        def _():
            lend4(hp).start()

        return 0

    def near3(hp, _):
        @pl.when(bit(1) == 0)
        def _():
            send3(hp).start()

        return 0

    def near2(hp, _):
        @pl.when(core == 0)
        def _():
            send2(hp).start()

        return 0

    lax.fori_loop(0, PAIRS, near2, 0)
    lax.fori_loop(0, PAIRS, near4, 0)
    lax.fori_loop(0, 4, near3, 0)
    rt[own] = ts[own]

    def wait_a():
        def one(h, _):
            @pl.when(h != own)
            def _():
                recv_a(h).wait_recv()
            return 0
        lax.fori_loop(0, 8, one, 0)
        i = lax.broadcasted_iota(jnp.int32, (512, 512), 0)
        j = lax.broadcasted_iota(jnp.int32, (512, 512), 1)
        i6, i7, i8 = i - 256, i - 384, i - 448
        at = jnp.where(i < 256, (i >> 5) * 64 + (i & 31),
             jnp.where(i < 384, (i6 >> 4) * 64 + 32 + (i6 & 15),
             jnp.where(i < 448, (i7 >> 3) * 64 + 48 + (i7 & 7),
             jnp.where(i < 480, (i8 >> 2) * 64 + 56 + (i8 & 3), -1))))
        move = jnp.where(at == j, 1.0, 0.0).astype(BF)
        both = jnp.concatenate([rt[:, 0].reshape(512, HEAD), rt[:, 1].reshape(512, HEAD)], axis=1)
        x = dot(move, both).astype(BF)
        xs[0] = x[:, :HEAD]
        xs[1] = x[:, HEAD:]
        for level in range(8, 4, -1):
            n = 1 << (level - 5)

            @pl.when(bit(level - 2) == 0)
            def _():
                for i in range(n):
                    copy_b(level, i).start()

    def wait_b():
        for level in range(8, 4, -1):
            n = 1 << (level - 5)

            @pl.when(bit(level - 2) == 1)
            def _():
                for i in range(n):
                    copy_b(level, i).wait_recv()
        tiles = []
        for level, ref in ((8, r8), (7, r7), (6, r6), (5, r5)):
            start = (0, 256, 384, 448)[level - 5]
            rows = 256 >> (level - 5)
            tiles.append(coarse_tile(
                level, lambda start=start, rows=rows: xs[0, start:start + rows, :],
                lambda ref=ref: ref[:, 0].reshape(256, HEAD), lambda ref=ref: ref[:, 1].reshape(256, HEAD),
                bit(level - 2) == 1, lambda *x, start=start, rows=rows: deep.__setitem__(
                    (slice(None), slice(start, start + rows)), jnp.stack(x))))
        run_tiles(tiles)
        deep_of = lambda start, rows: tuple(deep[i, start:start + rows, :] for i in range(3))
        state = deep_of(448, 32)
        for start, rows in ((384, 64), (256, 128), (0, 256)):
            state = merge(widen(state, wide.at[0], 2), deep_of(start, rows))
        lane = lax.broadcasted_iota(jnp.int32, (256, HEAD), 1)
        place = lax.broadcasted_iota(jnp.int32, (256, HEAD), 0) & 31
        stats = jnp.where(lane == place, state[1], jnp.where(lane == place + 32, state[2], 0.0))
        stats = jnp.sum(stats.reshape(8, 32, HEAD), axis=1, keepdims=True)
        cs[:, :32] = state[0].reshape(8, 32, HEAD)
        cs[:, 32:] = jnp.broadcast_to(stats, (8, 8, HEAD))
        cr[own] = cs[own]

        def one(h, _):
            @pl.when(h != own)
            def _():
                send_c(h).start()
            return 0
        lax.fori_loop(0, 8, one, 0)

    def local_pair(hp, _):
        @pl.when(core == 1)
        def _():
            send2(hp).wait_recv()
        tiles = []
        for e in range(2):
            cols = slice(e * HEAD, (e + 1) * HEAD)
            h = 2 * hp + e
            for seg in range(2):
                for half in range(2):
                    at, begin = seg * 512 + half * 256, seg * 512

                    def sink(num, peak, total, at=at, h=h):
                        base[h, 0, at:at + 256, :] = num * (1.0 / total)
                        lse = peak + jnp.log2(total) * (1.0 / C2)
                        base[h, 1, at:at + 256, :] = jnp.broadcast_to(lse, num.shape)

                    def parts(ref, begin=begin, half=half, cols=cols):
                        return [ref[hp, begin + i * 256:begin + (i + 1) * 256, cols] for i in range(half + 1)]

                    tiles.append({"q": lambda at=at, cols=cols: qb[hp, at:at + 256, cols],
                                  "k": lambda parts=parts: parts(kb), "v": lambda parts=parts: parts(vb),
                                  "bias": bias, "level": 0, "sink": sink})
            tiles.append(coarse_tile(1, lambda cols=cols: q1[hp, :, cols], lambda cols=cols: kv1[hp, 0, :, cols],
                                     lambda cols=cols: kv1[hp, 1, :, cols], None, store(near, h)))
            tiles.append(coarse_tile(2, lambda cols=cols: q2[hp, :, cols], lambda cols=cols: r2[hp, 0, :, cols],
                                     lambda cols=cols: r2[hp, 1, :, cols], core == 1, store(far, h)))
        run_tiles(tiles)
        forward4(hp)

        @pl.when(hp == 0)
        def _():
            wait_a()

        @pl.when(hp == 3)
        def _():
            wait_b()
        return 0

    lax.fori_loop(0, PAIRS, local_pair, 0)

    def out_copy(hp):
        cols = pl.ds(pl.multiple_of(hp * WIDE, WIDE), WIDE)
        return pltpu.make_async_copy(outb.at[hp], att_hbm.at[:, cols], out_sem.at[hp])

    def final_pair(step, _):
        @pl.when(step < PAIRS)
        def _():
            @pl.when(bit(2) == 1)
            def _():
                @pl.when(bit(1) == 0)
                def _():
                    recv4(step, 0).wait_recv()
                recv4(step, 1).wait_recv()
                relay4(step).start()

            @pl.when(bit(1) == 1)
            def _():
                send3(step).wait_recv()
                relay3(step).start()

        @pl.when(step > 0)
        def _():
            hp = step - 1

            @pl.when(bit(2) == 1)
            def _():
                copy_to(r4.at[hp, 1 - core], r4.at[hp, 1 - core], y4.at[hp], z4.at[hp], me ^ 1).wait_recv()

            @pl.when(bit(1) == 1)
            def _():
                copy_to(r3.at[hp, 1 - core], r3.at[hp, 1 - core], y3.at[hp], z3.at[hp], me ^ 1).wait_recv()

            tiles, threes, fours = [], [None] * 2, [None] * 2

            def keep(into, e):
                return lambda *x: into.__setitem__(e, x)

            for e in range(2):
                cols = slice(e * HEAD, (e + 1) * HEAD)
                tiles.append(coarse_tile(
                    4, lambda cols=cols: q4[hp, :, cols],
                    lambda cols=cols: r4[hp, :, :, 0, :, cols].reshape(256, HEAD),
                    lambda cols=cols: r4[hp, :, :, 1, :, cols].reshape(256, HEAD), bit(2) == 1, keep(fours, e)))
                tiles.append(coarse_tile(
                    3, lambda cols=cols: q3[hp, :, cols],
                    lambda cols=cols: r3[hp, :, 0, :, cols].reshape(256, HEAD),
                    lambda cols=cols: r3[hp, :, 1, :, cols].reshape(256, HEAD), bit(1) == 1, keep(threes, e)))
            run_tiles(tiles)
            for e in range(2):
                h = 2 * hp + e
                state = merge(widen(fours[e], wide.at[e], 2), threes[e])
                state = merge(widen(state, wide.at[e], 2), tuple(far[h, i] for i in range(3)))
                store(far, h)(*state)
        return 0

    lax.fori_loop(0, PAIRS + 1, final_pair, 0)

    def recv_c_all(h, _):
        @pl.when(h != own)
        def _():
            recv_c(h).wait_recv()
        return 0

    lax.fori_loop(0, 8, recv_c_all, 0)

    def last_pair(hp, _):
        r32 = lax.broadcasted_iota(jnp.int32, (32, HEAD), 0)
        l32 = lax.broadcasted_iota(jnp.int32, (32, HEAD), 1)
        states = []
        for e in range(2):
            h = 2 * hp + e
            stats = jnp.broadcast_to(cr[h, 32:33, :], (32, HEAD))
            column = lambda at: jnp.broadcast_to(
                jnp.sum(jnp.where(l32 == at, stats, 0.0), axis=1, keepdims=True), (32, HEAD))
            state = widen((cr[h, :32, :], column(r32), column(r32 + 32)), wide.at[e], 8)
            states.append(merge(state, tuple(far[h, i] for i in range(3))))
        for e in range(2):
            h = 2 * hp + e
            low = tuple(x[:128] for x in states[e])
            high = tuple(x[128:] for x in states[e])
            high = merge(widen(high, wide.at[e], 2, 512), tuple(near[h, i] for i in range(3)))
            for (num, peak, total), times, at in ((low, 4, 0), (high, 2, 512)):
                seen = total > 0.0
                safe = jnp.where(seen, total, 1.0)
                pair = (num * (1.0 / safe), jnp.where(seen, peak + jnp.log2(safe) * (1.0 / C2), NEG))
                coarse, lse = widen(pair, wide.at[e], times, at)
                fine, fine_lse = base[h, 0, at:at + 512, :], base[h, 1, at:at + 512, :]
                share = 1.0 / (1.0 + jnp.exp2((fine_lse - lse) * C2))
                outb[hp, at:at + 512, e * HEAD:(e + 1) * HEAD] = (fine + share * (coarse - fine)).astype(BF)
        out_copy(hp).start()
        return 0

    lax.fori_loop(0, PAIRS, last_pair, 0)

    def drain(hp, _):
        out_copy(hp).wait()

        @pl.when(core == 0)
        def _():
            send2(hp).wait_send()

        @pl.when(bit(1) == 0)
        def _():
            send3(hp).wait_send()

        @pl.when(bit(1) == 1)
        def _():
            relay3(hp).wait_send()

        @pl.when(bit(2) == 0)
        def _():
            send4(hp).wait_send()
            lend4(hp).wait_send()

        @pl.when(bit(2) == 1)
        def _():
            relay4(hp).wait_send()

        @pl.when(own >= 6)
        def _():
            hand4(hp).wait_send()
        return 0

    lax.fori_loop(0, PAIRS, drain, 0)

    def drain_octet(h, _):
        @pl.when(h != own)
        def _():
            send_a(h).wait_send()
            send_c(h).wait_send()
        return 0

    lax.fori_loop(0, 8, drain_octet, 0)
    for level in range(8, 4, -1):
        n = 1 << (level - 5)

        @pl.when(bit(level - 2) == 0)
        def _():
            for i in range(n):
                copy_b(level, i).wait_send()


def attend(queries, keys, values):
    count, width = queries.shape
    vm = lambda *shape: pltpu.VMEM(shape, BF)
    vf = lambda *shape: pltpu.VMEM(shape, F32)
    dma = lambda *shape: pltpu.SemaphoreType.DMA(shape)
    scratch = [
        vm(4, 1024, 256), vm(4, 1024, 256), vm(4, 1024, 256),
        vm(4, 304, 256), vf(256, 256),
        vm(4, 2, 256, 256), vm(4, 256, 256),
        vm(4, 2, 256, 256), vm(4, 256, 256), vm(4, 2, 256, 256),
        vm(4, 2, 128, 256), vm(4, 128, 256), vm(4, 2, 2, 128, 256),
        vm(4, 2, 64, 256), vm(4, 64, 256), vm(4, 2, 2, 2, 64, 256), vm(4, 2, 64, 256),
        vm(8, 2, 64, 128), vm(8, 2, 64, 128), vm(2, 512, 128),
        vm(1, 2, 256, 128), vm(2, 2, 128, 128), vm(4, 2, 64, 128), vm(8, 2, 32, 128),
        vf(8, 40, 128), vf(8, 40, 128),
        vf(2, 3, 1024, 128), vf(8, 2, 1024, 128),
        vf(8, 3, 256, 128), vf(8, 3, 256, 128), vf(3, 480, 128), vm(4, 1024, 256),
        dma(4, 3), dma(4),
        dma(4), dma(4),
        dma(4), dma(4), dma(4), dma(4),
        dma(4, 2), dma(4, 2), dma(4), dma(4), dma(4),
        dma(8), dma(8), dma(15), dma(15), dma(8), dma(8),
    ]
    return pl.pallas_call(
        kernel,
        out_shape=jax.ShapeDtypeStruct((count, width), BF),
        in_specs=[pl.BlockSpec(memory_space=pl.ANY)] * 3,
        out_specs=pl.BlockSpec(memory_space=pl.ANY),
        scratch_shapes=scratch,
        compiler_params=pltpu.CompilerParams(
            collective_id=0, has_side_effects=True, vmem_limit_bytes=50 * 1024 * 1024
        ),
        name="hierarchical_attention",
    )(queries, keys, values)


def on_device(queries, keys, values, w_out):
    attended = attend(queries, keys, values)
    return jnp.dot(attended, w_out, preferred_element_type=F32).astype(BF)


def solution(mesh):
    return jax.shard_map(
        on_device,
        mesh=mesh,
        in_specs=(P("seq", None), P("seq", None), P("seq", None), P()),
        out_specs=P("seq", None),
        check_vma=False,
    )
```

```python
import functools
import math

import jax
import jax.numpy as jnp
from jax import lax
from jax.experimental import pallas as pl
from jax.experimental.pallas import tpu as pltpu
from jax.sharding import PartitionSpec as P

MESH = pl.DeviceIdType.MESH
HEAD = 128
PAIRS = 4
WIDE = 256
NEG = -1e30
C2 = HEAD ** -0.5 * math.log2(math.e)
BF = jnp.bfloat16
F32 = jnp.float32


def nt_dot(a, b):
    return lax.dot_general(a, b, (((1,), (1,)), ((), ())), preferred_element_type=F32)


def dot(a, b):
    return lax.dot_general(a, b, (((1,), (0,)), ((), ())), preferred_element_type=F32)


def tile_scores(tile):
    q, keys = tile["q"](), tile["k"]()
    scores = [nt_dot(q, k) for k in keys]
    if tile["bias"] is not None:
        scores[-1] = scores[-1] + tile["bias"][...]
    return scores


def tile_probs(tile, scores):
    scale = C2 * 4.0 ** -tile["level"]
    peak = None
    for s in scores:
        top = jnp.max(s, axis=1, keepdims=True)
        peak = top if peak is None else jnp.maximum(peak, top)
    probs, total = [], None
    for s in scores:
        p = jnp.exp2((s - peak) * scale)
        row = jnp.sum(p, axis=1, keepdims=True)
        total = row if total is None else total + row
        probs.append(p.astype(BF))
    return probs, peak, total


def tile_out(tile, probs, peak, total):
    num = None
    for p, v in zip(probs, tile["v"]()):
        part = dot(p, v)
        num = part if num is None else num + part
    tile["sink"](num, peak, total)


def run_tiles(tiles):
    scores, probs = {}, {}
    count = len(tiles)
    for i in range(count + 2):
        if i < count:
            scores[i] = tile_scores(tiles[i])
        if 1 <= i <= count:
            probs[i - 1] = tile_probs(tiles[i - 1], scores.pop(i - 1))
        if i >= 2:
            tile_out(tiles[i - 2], *probs.pop(i - 2))


def coarse_tile(level, q, k, v, flag, sink):
    def done(num, peak, total):
        peak = jnp.broadcast_to(peak * 4.0 ** -level, num.shape)
        total = jnp.broadcast_to(total * 2.0 ** level, num.shape)
        if flag is not None:
            num = jnp.where(flag, num, 0.0)
            peak = jnp.where(flag, peak, NEG)
            total = jnp.where(flag, total, 0.0)
        sink(num, peak, total)
    return {"q": q, "k": lambda: [k()], "v": lambda: [v()], "bias": None, "level": level, "sink": done}


def store(ref, *index):
    def sink(*planes):
        for i, plane in enumerate(planes):
            ref[(*index, i)] = plane
    return sink


def merge(a, b):
    top = jnp.maximum(a[1], b[1])
    fa = jnp.exp2((a[1] - top) * C2)
    fb = jnp.exp2((b[1] - top) * C2)
    return fa * a[0] + fb * b[0], top, fa * a[2] + fb * b[2]


def widen(state, ref, times, start=0):
    rows = state[0].shape[0]
    for plane, value in enumerate(state):
        for r in range(times):
            ref[plane, pl.ds(start + r, rows, stride=times), :] = value
    return tuple(ref[i, pl.ds(start, rows * times), :] for i in range(len(state)))


def kernel(q_hbm, k_hbm, v_hbm, att_hbm, qb, kb, vb, pool, bias,
           kv1, q1, kv2, q2, r2, kv3, q3, r3, kv4, q4, r4, f4,
           ts, rt, xs, r5, r6, r7, r8, cs, cr, wide, base, near, far, deep, outb,
           load_sem, out_sem, s2, g2, s3, g3, y3, z3, s4, g4, h4, y4, z4,
           sa, ga, sb, gb, sc, gc):
    me = lax.axis_index("seq")
    core = me & 1
    own = me & 7
    octet = me - own

    def bit(i):
        return (me >> i) & 1

    def load(hp, t):
        src = (k_hbm, v_hbm, q_hbm)[t]
        dst = (kb, vb, qb)[t]
        cols = pl.ds(pl.multiple_of(hp * WIDE, WIDE), WIDE)
        return pltpu.make_async_copy(src.at[:, cols], dst.at[hp], load_sem.at[hp, t])

    for hp in range(PAIRS):
        for t in range(3):
            load(hp, t).start()

    barrier = pltpu.get_barrier_semaphore()
    masks = list(range(1, 8)) + [8 * o for o in range(1, 16)]

    def greet(i, _):
        mask = jnp.where(i < 8, i, (i - 7) * 8)
        pl.semaphore_signal(barrier, inc=1, device_id=(me ^ mask,), device_id_type=MESH)
        return 0

    lax.fori_loop(1, 23, greet, 0)

    row = lax.broadcasted_iota(jnp.int32, (304, WIDE), 0)
    col = lax.broadcasted_iota(jnp.int32, (304, WIDE), 1)
    tail = row >= 240
    shift = jnp.where(row < 128, 1, jnp.where(row < 192, 2, jnp.where(row < 224, 3, 4)))
    off = jnp.where(row < 128, row, jnp.where(row < 192, row - 128, jnp.where(row < 224, row - 192, row - 224)))
    t = row - 240
    shift_t = jnp.where(t < 32, 5, jnp.where(t < 48, 6, jnp.where(t < 56, 7, 8)))
    off_t = jnp.where(t < 32, t, jnp.where(t < 48, t - 32, jnp.where(t < 56, t - 48, t - 56)))
    shift = jnp.where(tail, shift_t, shift)
    off = jnp.where(tail, off_t, off)
    for i in range(4):
        at = jnp.where(tail, col + 256 * i, col)
        pool[i] = jnp.where((at >> shift) == off, 1.0, 0.0).astype(BF)
    r_i = lax.broadcasted_iota(jnp.int32, (256, 256), 0)
    c_i = lax.broadcasted_iota(jnp.int32, (256, 256), 1)
    bias[...] = jnp.where(c_i <= r_i, 0.0, NEG)

    tr = lax.broadcasted_iota(jnp.int32, (64, WIDE), 0)
    side = jnp.where(tr < 32, bit(3), jnp.where(tr < 48, bit(4), jnp.where(tr < 56, bit(5), bit(6))))

    def copy_to(src, dst, send, recv, device):
        return pltpu.make_async_remote_copy(src_ref=src, dst_ref=dst, send_sem=send, recv_sem=recv,
                                            device_id=(device,), device_id_type=MESH)

    def send2(hp):
        return copy_to(kv2.at[hp], r2.at[hp], s2.at[hp], g2.at[hp], me ^ 1)

    def send3(hp):
        return copy_to(kv3.at[hp], r3.at[hp, core], s3.at[hp], g3.at[hp], me ^ 2)

    def relay3(hp):
        return copy_to(r3.at[hp, core], r3.at[hp, core], y3.at[hp], z3.at[hp], me ^ 1)

    def send4(hp):
        return copy_to(kv4.at[hp], r4.at[hp, core, bit(1)], s4.at[hp, 0], g4.at[hp, 0], me ^ 6)

    def recv4(hp, j):
        return copy_to(kv4.at[hp], r4.at[hp, core, bit(1) ^ 1 ^ j], s4.at[hp, j], g4.at[hp, j], me ^ 6)

    def lend4(hp):
        return copy_to(kv4.at[hp], f4.at[hp], s4.at[hp, 1], h4.at[hp], me ^ 2)

    def pass4(hp):
        return copy_to(f4.at[hp], r4.at[hp, core, 1], s4.at[hp, 1], g4.at[hp, 1], me ^ 6)

    def hand4(hp):
        return copy_to(r4.at[hp, core, 0], r4.at[hp, core, 0], s4.at[hp, 0], g4.at[hp, 1], me ^ 2)

    def forward4(hp):
        @pl.when(own < 2)
        def _():
            lend4(hp).wait_recv()
            pass4(hp).start()

        @pl.when(own >= 6)
        def _():
            recv4(hp, 0).wait_recv()
            hand4(hp).start()

    def relay4(hp):
        return copy_to(r4.at[hp, core], r4.at[hp, core], y4.at[hp], z4.at[hp], me ^ 1)

    def send_a(h):
        return copy_to(ts.at[h], rt.at[own], sa.at[h], ga.at[own], octet + h)

    def recv_a(h):
        return copy_to(ts.at[h], rt.at[h], sa.at[h], ga.at[h], octet + h)

    def send_c(h):
        return copy_to(cs.at[h], cr.at[own], sc.at[h], gc.at[own], octet + h)

    def recv_c(h):
        return copy_to(cs.at[h], cr.at[h], sc.at[h], gc.at[h], octet + h)

    def copy_b(level, i):
        count = 256 >> (level - 5)
        start = (0, 256, 384, 448)[level - 5]
        n = 1 << (level - 5)
        dst = (r5, r6, r7, r8)[level - 5]
        slot = n - 1 + i
        mask = 8 * (n + i)
        return copy_to(xs.at[:, pl.ds(start, count)], dst.at[i], sb.at[slot], gb.at[slot], me ^ mask)

    def octet_sends(h, _):
        @pl.when(h != own)
        def _():
            send_a(h).start()
        return 0

    def pool_pair(hp, _):
        @pl.when(hp == 3)
        def _():
            pl.semaphore_wait(barrier, len(masks))
            lax.fori_loop(0, 6, octet_sends, 0)

        tails = []
        for t in range(3):
            load(hp, t).wait()
            src = (kb, vb, qb)[t]
            acc = None
            ys = {}
            for step in range(5):
                if step < 4:
                    start = 0 if (step < 2) == (t < 2) else 128
                    ys[step] = (start, dot(pool[step, start:], src[hp, step * 256:(step + 1) * 256, :]))
                if step == 0:
                    continue
                i = step - 1
                start, y = ys.pop(i)
                yb = y[:240 - start].astype(BF)
                mid = 128 - start
                if start == 0:
                    if t < 2:
                        kv1[hp, t, i * 128:(i + 1) * 128, :] = yb[:128]
                    else:
                        q1[hp, (i - 2) * 128:(i - 1) * 128, :] = yb[:128]
                if t < 2:
                    kv2[hp, t, i * 64:(i + 1) * 64, :] = yb[mid:mid + 64]
                    kv3[hp, t, i * 32:(i + 1) * 32, :] = yb[mid + 64:mid + 96]
                    kv4[hp, t, i * 16:(i + 1) * 16, :] = yb[mid + 96:mid + 112]
                else:
                    q2[hp, i * 64:(i + 1) * 64, :] = yb[mid:mid + 64]
                    q3[hp, i * 32:(i + 1) * 32, :] = yb[mid + 64:mid + 96]
                    q4[hp, i * 16:(i + 1) * 16, :] = yb[mid + 96:mid + 112]
                acc = y[mid + 112:] if acc is None else acc + y[mid + 112:]
            tails.append(acc)

        first = jnp.where(side == 0, tails[0], tails[2]).astype(BF)
        second = tails[1].astype(BF)
        for e in range(2):
            h = 2 * hp + e
            ts[h, 0] = first[:, e * HEAD:(e + 1) * HEAD]
            ts[h, 1] = second[:, e * HEAD:(e + 1) * HEAD]

        return 0

    lax.fori_loop(0, PAIRS, pool_pair, 0)
    lax.fori_loop(6, 8, octet_sends, 0)

    def near4(hp, _):
        @pl.when(bit(2) == 0)
        def _():
            send4(hp).start()

        @pl.when((own & 6) == 2)
        def _():
            lend4(hp).start()

        return 0

    def near3(hp, _):
        @pl.when(bit(1) == 0)
        def _():
            send3(hp).start()

        return 0

    def near2(hp, _):
        @pl.when(core == 0)
        def _():
            send2(hp).start()

        return 0

    lax.fori_loop(0, PAIRS, near2, 0)
    lax.fori_loop(0, PAIRS, near4, 0)
    lax.fori_loop(0, 4, near3, 0)
    rt[own] = ts[own]

    def wait_a():
        def one(h, _):
            @pl.when(h != own)
            def _():
                recv_a(h).wait_recv()
            return 0
        lax.fori_loop(0, 8, one, 0)
        i = lax.broadcasted_iota(jnp.int32, (512, 512), 0)
        j = lax.broadcasted_iota(jnp.int32, (512, 512), 1)
        i6, i7, i8 = i - 256, i - 384, i - 448
        at = jnp.where(i < 256, (i >> 5) * 64 + (i & 31),
             jnp.where(i < 384, (i6 >> 4) * 64 + 32 + (i6 & 15),
             jnp.where(i < 448, (i7 >> 3) * 64 + 48 + (i7 & 7),
             jnp.where(i < 480, (i8 >> 2) * 64 + 56 + (i8 & 3), -1))))
        move = jnp.where(at == j, 1.0, 0.0).astype(BF)
        both = jnp.concatenate([rt[:, 0].reshape(512, HEAD), rt[:, 1].reshape(512, HEAD)], axis=1)
        x = dot(move, both).astype(BF)
        xs[0] = x[:, :HEAD]
        xs[1] = x[:, HEAD:]
        for level in range(8, 4, -1):
            n = 1 << (level - 5)

            @pl.when(bit(level - 2) == 0)
            def _():
                for i in range(n):
                    copy_b(level, i).start()

    def wait_b():
        for level in range(8, 4, -1):
            n = 1 << (level - 5)

            @pl.when(bit(level - 2) == 1)
            def _():
                for i in range(n):
                    copy_b(level, i).wait_recv()
        tiles = []
        for level, ref in ((8, r8), (7, r7), (6, r6), (5, r5)):
            start = (0, 256, 384, 448)[level - 5]
            rows = 256 >> (level - 5)
            tiles.append(coarse_tile(
                level, lambda start=start, rows=rows: xs[0, start:start + rows, :],
                lambda ref=ref: ref[:, 0].reshape(256, HEAD), lambda ref=ref: ref[:, 1].reshape(256, HEAD),
                bit(level - 2) == 1, lambda *x, start=start, rows=rows: deep.__setitem__(
                    (slice(None), slice(start, start + rows)), jnp.stack(x))))
        run_tiles(tiles)
        deep_of = lambda start, rows: tuple(deep[i, start:start + rows, :] for i in range(3))
        state = deep_of(448, 32)
        for start, rows in ((384, 64), (256, 128), (0, 256)):
            state = merge(widen(state, wide.at[0], 2), deep_of(start, rows))
        lane = lax.broadcasted_iota(jnp.int32, (256, HEAD), 1)
        place = lax.broadcasted_iota(jnp.int32, (256, HEAD), 0) & 31
        stats = jnp.where(lane == place, state[1], jnp.where(lane == place + 32, state[2], 0.0))
        stats = jnp.sum(stats.reshape(8, 32, HEAD), axis=1, keepdims=True)
        cs[:, :32] = state[0].reshape(8, 32, HEAD)
        cs[:, 32:] = jnp.broadcast_to(stats, (8, 8, HEAD))
        cr[own] = cs[own]

        def one(h, _):
            @pl.when(h != own)
            def _():
                send_c(h).start()
            return 0
        lax.fori_loop(0, 8, one, 0)

    def local_pair(hp, _):
        @pl.when(core == 1)
        def _():
            send2(hp).wait_recv()
        tiles = []
        for e in range(2):
            cols = slice(e * HEAD, (e + 1) * HEAD)
            h = 2 * hp + e
            for seg in range(2):
                for half in range(2):
                    at, begin = seg * 512 + half * 256, seg * 512

                    def sink(num, peak, total, at=at, h=h):
                        base[h, 0, at:at + 256, :] = num * (1.0 / total)
                        lse = peak + jnp.log2(total) * (1.0 / C2)
                        base[h, 1, at:at + 256, :] = jnp.broadcast_to(lse, num.shape)

                    def parts(ref, begin=begin, half=half, cols=cols):
                        return [ref[hp, begin + i * 256:begin + (i + 1) * 256, cols] for i in range(half + 1)]

                    tiles.append({"q": lambda at=at, cols=cols: qb[hp, at:at + 256, cols],
                                  "k": lambda parts=parts: parts(kb), "v": lambda parts=parts: parts(vb),
                                  "bias": bias, "level": 0, "sink": sink})
            tiles.append(coarse_tile(1, lambda cols=cols: q1[hp, :, cols], lambda cols=cols: kv1[hp, 0, :, cols],
                                     lambda cols=cols: kv1[hp, 1, :, cols], None, store(near, h)))
            tiles.append(coarse_tile(2, lambda cols=cols: q2[hp, :, cols], lambda cols=cols: r2[hp, 0, :, cols],
                                     lambda cols=cols: r2[hp, 1, :, cols], core == 1, store(far, h)))
        run_tiles(tiles)
        forward4(hp)

        @pl.when(hp == 0)
        def _():
            wait_a()

        @pl.when(hp == 3)
        def _():
            wait_b()
        return 0

    lax.fori_loop(0, PAIRS, local_pair, 0)

    def out_copy(hp):
        cols = pl.ds(pl.multiple_of(hp * WIDE, WIDE), WIDE)
        return pltpu.make_async_copy(outb.at[hp], att_hbm.at[:, cols], out_sem.at[hp])

    def final_pair(step, _):
        @pl.when(step < PAIRS)
        def _():
            @pl.when(bit(2) == 1)
            def _():
                @pl.when(bit(1) == 0)
                def _():
                    recv4(step, 0).wait_recv()
                recv4(step, 1).wait_recv()
                relay4(step).start()

            @pl.when(bit(1) == 1)
            def _():
                send3(step).wait_recv()
                relay3(step).start()

        @pl.when(step > 0)
        def _():
            hp = step - 1

            @pl.when(bit(2) == 1)
            def _():
                copy_to(r4.at[hp, 1 - core], r4.at[hp, 1 - core], y4.at[hp], z4.at[hp], me ^ 1).wait_recv()

            @pl.when(bit(1) == 1)
            def _():
                copy_to(r3.at[hp, 1 - core], r3.at[hp, 1 - core], y3.at[hp], z3.at[hp], me ^ 1).wait_recv()

            tiles, threes, fours = [], [None] * 2, [None] * 2

            def keep(into, e):
                return lambda *x: into.__setitem__(e, x)

            for e in range(2):
                cols = slice(e * HEAD, (e + 1) * HEAD)
                tiles.append(coarse_tile(
                    4, lambda cols=cols: q4[hp, :, cols],
                    lambda cols=cols: r4[hp, :, :, 0, :, cols].reshape(256, HEAD),
                    lambda cols=cols: r4[hp, :, :, 1, :, cols].reshape(256, HEAD), bit(2) == 1, keep(fours, e)))
                tiles.append(coarse_tile(
                    3, lambda cols=cols: q3[hp, :, cols],
                    lambda cols=cols: r3[hp, :, 0, :, cols].reshape(256, HEAD),
                    lambda cols=cols: r3[hp, :, 1, :, cols].reshape(256, HEAD), bit(1) == 1, keep(threes, e)))
            run_tiles(tiles)
            for e in range(2):
                h = 2 * hp + e
                state = merge(widen(fours[e], wide.at[e], 2), threes[e])
                state = merge(widen(state, wide.at[e], 2), tuple(far[h, i] for i in range(3)))
                store(far, h)(*state)
        return 0

    lax.fori_loop(0, PAIRS + 1, final_pair, 0)

    def recv_c_all(h, _):
        @pl.when(h != own)
        def _():
            recv_c(h).wait_recv()
        return 0

    lax.fori_loop(0, 8, recv_c_all, 0)

    def last_pair(hp, _):
        r32 = lax.broadcasted_iota(jnp.int32, (32, HEAD), 0)
        l32 = lax.broadcasted_iota(jnp.int32, (32, HEAD), 1)
        states = []
        for e in range(2):
            h = 2 * hp + e
            stats = jnp.broadcast_to(cr[h, 32:33, :], (32, HEAD))
            column = lambda at: jnp.broadcast_to(
                jnp.sum(jnp.where(l32 == at, stats, 0.0), axis=1, keepdims=True), (32, HEAD))
            state = widen((cr[h, :32, :], column(r32), column(r32 + 32)), wide.at[e], 8)
            states.append(merge(state, tuple(far[h, i] for i in range(3))))
        for e in range(2):
            h = 2 * hp + e
            low = tuple(x[:128] for x in states[e])
            high = tuple(x[128:] for x in states[e])
            high = merge(widen(high, wide.at[e], 2, 512), tuple(near[h, i] for i in range(3)))
            for (num, peak, total), times, at in ((low, 4, 0), (high, 2, 512)):
                seen = total > 0.0
                safe = jnp.where(seen, total, 1.0)
                pair = (num * (1.0 / safe), jnp.where(seen, peak + jnp.log2(safe) * (1.0 / C2), NEG))
                coarse, lse = widen(pair, wide.at[e], times, at)
                fine, fine_lse = base[h, 0, at:at + 512, :], base[h, 1, at:at + 512, :]
                share = 1.0 / (1.0 + jnp.exp2((fine_lse - lse) * C2))
                outb[hp, at:at + 512, e * HEAD:(e + 1) * HEAD] = (fine + share * (coarse - fine)).astype(BF)
        out_copy(hp).start()
        return 0

    lax.fori_loop(0, PAIRS, last_pair, 0)

    def drain(hp, _):
        out_copy(hp).wait()

        @pl.when(core == 0)
        def _():
            send2(hp).wait_send()

        @pl.when(bit(1) == 0)
        def _():
            send3(hp).wait_send()

        @pl.when(bit(1) == 1)
        def _():
            relay3(hp).wait_send()

        @pl.when(bit(2) == 0)
        def _():
            send4(hp).wait_send()
            lend4(hp).wait_send()

        @pl.when(bit(2) == 1)
        def _():
            relay4(hp).wait_send()

        @pl.when(own >= 6)
        def _():
            hand4(hp).wait_send()
        return 0

    lax.fori_loop(0, PAIRS, drain, 0)

    def drain_octet(h, _):
        @pl.when(h != own)
        def _():
            send_a(h).wait_send()
            send_c(h).wait_send()
        return 0

    lax.fori_loop(0, 8, drain_octet, 0)
    for level in range(8, 4, -1):
        n = 1 << (level - 5)

        @pl.when(bit(level - 2) == 0)
        def _():
            for i in range(n):
                copy_b(level, i).wait_send()


def attend(queries, keys, values):
    count, width = queries.shape
    vm = lambda *shape: pltpu.VMEM(shape, BF)
    vf = lambda *shape: pltpu.VMEM(shape, F32)
    dma = lambda *shape: pltpu.SemaphoreType.DMA(shape)
    scratch = [
        vm(4, 1024, 256), vm(4, 1024, 256), vm(4, 1024, 256),
        vm(4, 304, 256), vf(256, 256),
        vm(4, 2, 256, 256), vm(4, 256, 256),
        vm(4, 2, 256, 256), vm(4, 256, 256), vm(4, 2, 256, 256),
        vm(4, 2, 128, 256), vm(4, 128, 256), vm(4, 2, 2, 128, 256),
        vm(4, 2, 64, 256), vm(4, 64, 256), vm(4, 2, 2, 2, 64, 256), vm(4, 2, 64, 256),
        vm(8, 2, 64, 128), vm(8, 2, 64, 128), vm(2, 512, 128),
        vm(1, 2, 256, 128), vm(2, 2, 128, 128), vm(4, 2, 64, 128), vm(8, 2, 32, 128),
        vf(8, 40, 128), vf(8, 40, 128),
        vf(2, 3, 1024, 128), vf(8, 2, 1024, 128),
        vf(8, 3, 256, 128), vf(8, 3, 256, 128), vf(3, 480, 128), vm(4, 1024, 256),
        dma(4, 3), dma(4),
        dma(4), dma(4),
        dma(4), dma(4), dma(4), dma(4),
        dma(4, 2), dma(4, 2), dma(4), dma(4), dma(4),
        dma(8), dma(8), dma(15), dma(15), dma(8), dma(8),
    ]
    return pl.pallas_call(
        kernel,
        out_shape=jax.ShapeDtypeStruct((count, width), BF),
        in_specs=[pl.BlockSpec(memory_space=pl.ANY)] * 3,
        out_specs=pl.BlockSpec(memory_space=pl.ANY),
        scratch_shapes=scratch,
        compiler_params=pltpu.CompilerParams(
            collective_id=0, has_side_effects=True, vmem_limit_bytes=50 * 1024 * 1024
        ),
        name="hierarchical_attention",
    )(queries, keys, values)


def on_device(queries, keys, values, w_out):
    attended = attend(queries, keys, values)
    return jnp.dot(attended, w_out, preferred_element_type=F32).astype(BF)


def solution(mesh):
    return jax.shard_map(
        on_device,
        mesh=mesh,
        in_specs=(P("seq", None), P("seq", None), P("seq", None), P()),
        out_specs=P("seq", None),
        check_vma=False,
    )
```
